32 devices in a mesh: section: 2 (over y), ctx: 16 (over z, x, core), tp: 1.
Axes of the slice: x: 2, y: 2, z: 4, core: 2. Of those that a mesh axis runs over, the one named last changes fastest.
Arguments:
- query_heads: bfloat16 [2, 2, 2048, 6144], P('section', None, 'ctx', 'tp'), may hold values from -8 to 8
- keys_values: bfloat16 [2, 2048, 2, 1024], P('section', 'ctx', None, 'tp'), may hold values from -12 to 12
- grad_output: bfloat16 [2, 2, 2048, 6144], P('section', None, 'ctx', 'tp'), may hold values from -6 to 6
- norm_gain: float32 [2, 2, 6144], P('section', None, 'tp'), may hold values from 0.1 to 1.9
- turn_ids: int32 [2048], P('ctx'), may hold values from 0 to 63, never falling along the last dimension, each value on 1 to 64 neighbouring positions
Outputs:
- normed_out: bfloat16 [2, 2, 2048, 6144], P('section', None, 'ctx', 'tp')
- query_grad: bfloat16 [2, 2, 2048, 6144], P('section', None, 'ctx', 'tp')
- kv_grad: float32 [2, 2048, 2, 1024], P('section', 'ctx', None, 'tp')
The draws below stay inside these ranges and needn't reach their ends.
Inputs may be any that keep to these rules, and one draw needn't show every extreme that they name: `turn_ids`: turn numbers never fall along the dialogue; a turn holds 1 to 64 positions and one holds exactly 64; every turn number occurs.
All inputs are finite; a program needn't handle non-finite values.
Results may differ from the reference program's by a relative error of at most 0.015.
Values may be sent and summed in bfloat16 or wider, within the bound.
A program may use at most 128 MiB of HBM per device.

```python
import math
import jax
import jax.numpy as jnp
import numpy as np
from jax import lax

HD = 128
KVH = 8
GROUP = 6
HQ = 48
SEQ = 2048
SECTIONS = 2
TURNS = 64
TURN_MOST = 64


def draw_query_heads(key, part):
    shape_full = (SECTIONS, 2, SEQ, KVH, GROUP, HD)
    drawn = jax.random.normal(jax.random.fold_in(key, 11), shape_full, jnp.float32)
    drawn = jnp.clip(drawn, -8.0, 8.0)
    return drawn.reshape(SECTIONS, 2, SEQ, KVH * GROUP * HD).astype(jnp.bfloat16)


def draw_keys_values(key, part):
    shape_half = (SECTIONS, SEQ, KVH, HD)
    ladder = jnp.arange(KVH, dtype=jnp.float32) / (KVH - 1)
    key_part = jax.random.normal(jax.random.fold_in(key, 21), shape_half, jnp.float32)
    value_part = jax.random.normal(jax.random.fold_in(key, 22), shape_half, jnp.float32)
    head_scale = 0.3 * 10.0 ** ladder
    value_part = value_part * head_scale[None, None, :, None]
    stacked = jnp.clip(jnp.stack([key_part, value_part], axis=2), -12.0, 12.0)
    return stacked.reshape(SECTIONS, SEQ, 2, KVH * HD).astype(jnp.bfloat16)


def steps_of(stream_key, shape, split, least, top_value):
    def one(axis_at, parts):
        steps = jax.random.uniform(jax.random.fold_in(jax.random.fold_in(stream_key, 6), axis_at), (parts,), jnp.float32, least / len(split), top_value / len(split))
        return jnp.repeat(jnp.exp(steps), shape[axis_at] // parts).reshape((-1,) + (1,) * (len(shape) - axis_at - 1))

    factor_of = one(*split[0])
    for cut in split[1:]:
        factor_of = factor_of * one(*cut)
    return factor_of


def split_up(count, total, limit, slope):
    weights = [(1 << 20) // math.isqrt(standing ** slope) + 1 for standing in range(2, count + 1)]
    surplus, holding = total - limit - (count - 1), [1] * (count - 1)
    while surplus > 0:
        movable = [i for i in range(count - 1) if holding[i] < limit]
        mass, remaining = sum([weights[i] for i in movable]), surplus
        for i in movable:
            addition = min(limit - holding[i], max(1, remaining * weights[i] // mass), surplus)
            holding[i] = holding[i] + addition
            surplus = surplus - addition
    return np.array([limit] + holding)


def ragged(stream_key, number_of, total, bound, skew):
    if number_of == 2:
        one = jax.random.randint(stream_key, (), max(1, total - bound), min(bound, total - 1) + 1)
        return jnp.stack([one, total - one])
    lengths = jnp.asarray(split_up(number_of, total, bound, skew), jnp.int32)
    pairs = (number_of - 1) // 2
    giver, sink = lengths[1:1 + 2 * pairs:2], lengths[2:2 + 2 * pairs:2]
    room = jnp.minimum(giver - 1, bound - sink)
    passed = jax.random.randint(jax.random.fold_in(stream_key, 1), (pairs,), 0, 1 << 20) % (room + 1)
    lengths = lengths.at[1:1 + 2 * pairs:2].set(giver - passed).at[2:2 + 2 * pairs:2].set(sink + passed)
    return lengths[jax.random.permutation(jax.random.fold_in(stream_key, 2), number_of)]


def centred(stream_key, shape, width, bound, cuts=(), kind=jnp.bfloat16):
    gain = steps_of(stream_key, shape, cuts, -0.22, 0.18) if cuts else 1.0
    result = jax.random.normal(stream_key, shape, jnp.float32) * width * gain
    return jnp.minimum(jnp.maximum(result, -bound), bound).astype(kind)


def setup_inputs(seed: int = 0) -> dict:
    streams_of = jax.random.split(jax.random.key(seed), 6)
    return {
        "query_heads": draw_query_heads(jax.random.fold_in(streams_of[5], 71), 0),
        "keys_values": draw_keys_values(jax.random.fold_in(streams_of[5], 71), 0),
        "grad_output": centred(streams_of[2], (SECTIONS, 2, SEQ, HQ * HD), 1.0, 6.0, ((0, 2), (2, 16))),
        "norm_gain": jnp.clip(1.0 + 0.18 * jax.random.normal(streams_of[3], (SECTIONS, 2, HQ * HD), jnp.float32), 0.1, 1.9),
        "turn_ids": jnp.searchsorted(jnp.cumsum(ragged(streams_of[4], TURNS, SEQ, TURN_MOST, 2)), jnp.arange(SEQ), side="right").astype(jnp.int32),
    }


neg_big = -1e+30
eps_norm = 1e-06

def round_trip(values):
    return lax.optimization_barrier(values.astype(jnp.bfloat16)).astype(jnp.float32)

def head_weights(query_head, key_head, visible):
    scores = jnp.einsum('qgd,kd->gqk', query_head.astype(jnp.float32), key_head.astype(jnp.float32)) * HD ** (-0.5)
    row_max = lax.optimization_barrier(jnp.max(jnp.where(visible, scores, neg_big), axis=-1))
    weights = jnp.where(visible, jnp.exp(scores - row_max[..., None]), 0.0)
    return (weights, lax.optimization_barrier(jnp.sum(weights, axis=-1)))

def one_layer(query_flat, kv_rows, gain_vector, cotangent_flat, turn_rows):
    positions = jnp.arange(SEQ, dtype=jnp.int32)
    visible = (positions[None, :] <= positions[:, None]) | (turn_rows[None, :] == turn_rows[:, None])
    queries = query_flat.reshape(SEQ, KVH, GROUP, HD).transpose(1, 0, 2, 3)
    key_rows = kv_rows[:, 0].reshape(SEQ, KVH, HD).transpose(1, 0, 2)
    value_rows = kv_rows[:, 1].reshape(SEQ, KVH, HD).transpose(1, 0, 2)

    def forward_head(pieces):
        query_head, key_head, value_head = pieces
        weights, totals = head_weights(query_head, key_head, visible)
        mixture = jnp.einsum('gqk,kd->qgd', round_trip(weights), value_head.astype(jnp.float32))
        return mixture / jnp.transpose(totals)[..., None]
    output = lax.map(forward_head, (queries, key_rows, value_rows))
    output = jnp.transpose(output, (1, 0, 2, 3)).reshape(SEQ, KVH * GROUP * HD)
    inverse = lax.rsqrt(lax.optimization_barrier(jnp.mean(output * output, axis=-1)) + eps_norm)
    normed = (output * inverse[:, None] * gain_vector).astype(jnp.bfloat16)
    scaled = cotangent_flat.astype(jnp.float32) * gain_vector
    center = lax.optimization_barrier(jnp.mean(scaled * output, axis=-1))
    out_grad = round_trip(inverse[:, None] * (scaled - output * (inverse * inverse * center)[:, None]))
    grad_rows = out_grad.reshape(SEQ, KVH, GROUP, HD).transpose(1, 0, 2, 3)
    out_rows = output.reshape(SEQ, KVH, GROUP, HD).transpose(1, 0, 2, 3)

    def backward_head(pieces):
        query_head, key_head, value_head, grad_head, out_head = pieces
        weights, totals = head_weights(query_head, key_head, visible)
        chances = weights / totals[..., None]
        row_dot = jnp.transpose(lax.optimization_barrier(jnp.sum(grad_head * out_head, axis=-1)))
        value_grad = jnp.einsum('gqk,qgd->kd', round_trip(chances), grad_head)
        prob_grad = jnp.einsum('qgd,kd->gqk', grad_head, value_head.astype(jnp.float32))
        score_grad = round_trip(chances * (prob_grad - row_dot[..., None]))
        query_part = jnp.einsum('gqk,kd->qgd', score_grad, key_head.astype(jnp.float32)) * HD ** (-0.5)
        key_grad = jnp.einsum('gqk,qgd->kd', score_grad, query_head.astype(jnp.float32)) * HD ** (-0.5)
        return (query_part, jnp.stack([key_grad, value_grad], axis=1))
    query_part, kv_part = lax.map(backward_head, (queries, key_rows, value_rows, grad_rows, out_rows))
    query_part = jnp.transpose(query_part, (1, 0, 2, 3)).reshape(SEQ, KVH * GROUP * HD).astype(jnp.bfloat16)
    kv_part = jnp.transpose(kv_part, (1, 2, 0, 3)).reshape(SEQ, 2, KVH * HD)
    return (normed, query_part, kv_part)

def reference(query_heads, keys_values, grad_output, norm_gain, turn_ids):
    normed_all = []
    qgrad_all = []
    produced = []
    consumed = []
    for section_index in range(SECTIONS):
        producer = one_layer(query_heads[section_index, 0], keys_values[section_index], norm_gain[section_index, 0], grad_output[section_index, 0], turn_ids)
        consumer = one_layer(query_heads[section_index, 1], keys_values[(section_index - 1) % SECTIONS], norm_gain[section_index, 1], grad_output[section_index, 1], turn_ids)
        normed_all.append(jnp.stack([producer[0], consumer[0]]))
        qgrad_all.append(jnp.stack([producer[1], consumer[1]]))
        produced.append(producer[2])
        consumed.append(consumer[2])
    kv_grad = jnp.stack([produced[section_index] + consumed[(section_index + 1) % SECTIONS] for section_index in range(SECTIONS)])
    return (jnp.stack(normed_all), jnp.stack(qgrad_all), kv_grad)
```

```python
import jax
import jax.numpy as jnp
from jax import lax
from jax.experimental import pallas as pl
from jax.experimental.pallas import tpu as pltpu
from jax.sharding import PartitionSpec as P

HD = 128
KVH = 8
GROUP = 6


neg_big = -1e30
eps_norm = 1e-06
LOG2E = 1.4426950408889634
SPAN = 512


def dot_nn(a, b):
    return jnp.dot(a, b, preferred_element_type=jnp.float32)


def dot_nt(a, b):
    return lax.dot_general(a, b, (((1,), (1,)), ((), ())), preferred_element_type=jnp.float32)


def passed_along(block, axis, distance):
    devices = range(lax.axis_size(axis))
    route = [((i - distance) % len(devices), i) for i in devices]
    return lax.ppermute(block, axis, route)


def visible_mask(query_pos, query_seg, key_pos, key_seg):
    return (key_pos[None, :] <= query_pos[:, None]) | (key_seg[None, :] == query_seg[:, None])


def block_terms(queries, kv_rows, scaling):
    row_count = kv_rows.shape[0]
    head_count = queries.shape[1]
    key_rows = kv_rows[:, 0].reshape(row_count, head_count, HD)
    value_rows = kv_rows[:, 1].reshape(row_count, head_count, HD)
    scores = (
        jnp.einsum("qhgd,khd->hgqk", queries, key_rows, preferred_element_type=jnp.float32)
        * scaling
    )
    return (scores, key_rows, value_rows)


def run_layer(queries_flat, gathered, key_seg, query_pos, query_seg, gain_vector, cotangent_flat):
    tokens_here = queries_flat.shape[0]
    head_count = gathered.shape[2] // HD
    queries = queries_flat.reshape(tokens_here, head_count, GROUP, HD)
    scaling = HD ** (-0.5)
    seq_len = gathered.shape[0]
    span_rows = min(512, seq_len)
    blocks = seq_len // span_rows

    def block_view(number):
        offset = number * span_rows
        kv_rows = lax.dynamic_slice_in_dim(gathered, offset, span_rows, 0)
        key_pos = offset + jnp.arange(span_rows, dtype=jnp.int32)
        visible = visible_mask(
            query_pos, query_seg, key_pos, lax.dynamic_slice_in_dim(key_seg, offset, span_rows, 0)
        )
        scores, key_rows, value_rows = block_terms(queries, kv_rows, scaling)
        return (scores, key_rows, value_rows, visible)

    def forward_step(running, number):
        run_max, run_sum, accumulated = running
        scores, key_rows, value_rows, visible = block_view(number)
        new_max = jnp.maximum(run_max, jnp.max(jnp.where(visible, scores, neg_big), axis=-1))
        weights = jnp.where(visible, jnp.exp(scores - new_max[..., None]), 0.0)
        factor = jnp.exp(run_max - new_max)
        run_sum = run_sum * factor + jnp.sum(weights, axis=-1)
        update = jnp.einsum(
            "hgqk,khd->qhgd",
            weights.astype(jnp.bfloat16),
            value_rows,
            preferred_element_type=jnp.float32,
        )
        accumulated = accumulated * jnp.transpose(factor, (2, 0, 1))[..., None] + update
        return ((new_max, run_sum, accumulated), None)

    start_state = (
        jnp.full((head_count, GROUP, tokens_here), neg_big, jnp.float32),
        jnp.zeros((head_count, GROUP, tokens_here), jnp.float32),
        jnp.zeros((tokens_here, head_count, GROUP, HD), jnp.float32),
    )
    (row_max, row_sum, accumulated), unused = lax.scan(
        forward_step, start_state, jnp.arange(blocks, dtype=jnp.int32)
    )
    output = accumulated / jnp.transpose(row_sum, (2, 0, 1))[..., None]
    gain_grid = gain_vector.reshape(head_count, GROUP, HD)
    scaled = (
        cotangent_flat.reshape(tokens_here, head_count, GROUP, HD).astype(jnp.float32) * gain_grid
    )
    local_sq = jnp.sum(output * output, axis=(1, 2, 3))
    local_dot = jnp.sum(scaled * output, axis=(1, 2, 3))
    total_sq, total_dot = lax.psum((local_sq, local_dot), "tp")
    features = KVH * GROUP * HD
    inverse = lax.rsqrt(total_sq / features + eps_norm)
    normed = (output * inverse[:, None, None, None] * gain_grid).astype(jnp.bfloat16)
    center = total_dot / features
    out_grad = (
        inverse[:, None, None, None]
        * (scaled - output * (inverse * inverse * center)[:, None, None, None])
    ).astype(jnp.bfloat16)
    row_dot = jnp.transpose(jnp.sum(out_grad.astype(jnp.float32) * output, axis=-1), (1, 2, 0))

    def backward_step(grad_q, number):
        scores, key_rows, value_rows, visible = block_view(number)
        chances = jnp.where(visible, jnp.exp(scores - row_max[..., None]), 0.0) / row_sum[..., None]
        value_grad = jnp.einsum(
            "hgqk,qhgd->khd",
            chances.astype(jnp.bfloat16),
            out_grad,
            preferred_element_type=jnp.float32,
        )
        prob_grad = jnp.einsum(
            "qhgd,khd->hgqk", out_grad, value_rows, preferred_element_type=jnp.float32
        )
        score_grad = (chances * (prob_grad - row_dot[..., None])).astype(jnp.bfloat16)
        grad_q = (
            grad_q
            + jnp.einsum("hgqk,khd->qhgd", score_grad, key_rows, preferred_element_type=jnp.float32)
            * scaling
        )
        key_grad = (
            jnp.einsum("hgqk,qhgd->khd", score_grad, queries, preferred_element_type=jnp.float32)
            * scaling
        )
        return (grad_q, jnp.stack([key_grad, value_grad], axis=1))

    grad_q, pieces = lax.scan(
        backward_step,
        jnp.zeros((tokens_here, head_count, GROUP, HD), jnp.float32),
        jnp.arange(blocks, dtype=jnp.int32),
    )
    kv_partial = pieces.reshape(seq_len, 2, head_count * HD)
    return (
        normed.reshape(tokens_here, -1),
        grad_q.reshape(tokens_here, -1).astype(jnp.bfloat16),
        kv_partial,
    )


def on_device(query_heads, keys_values, grad_output, norm_gain, turn_ids):
    tokens_here = turn_ids.shape[0]
    query_pos = lax.axis_index("ctx") * tokens_here + jnp.arange(tokens_here, dtype=jnp.int32)
    own_rows = keys_values[0]
    earlier = passed_along(own_rows, "section", 1)
    own_full, key_seg = (
        lax.all_gather(own_rows, "ctx", axis=0, tiled=True),
        lax.all_gather(turn_ids, "ctx", axis=0, tiled=True),
    )
    earlier_full = lax.all_gather(earlier, "ctx", axis=0, tiled=True)
    producer = run_layer(
        query_heads[0, 0],
        own_full,
        key_seg,
        query_pos,
        turn_ids,
        norm_gain[0, 0],
        grad_output[0, 0],
    )
    consumer = run_layer(
        query_heads[0, 1],
        earlier_full,
        key_seg,
        query_pos,
        turn_ids,
        norm_gain[0, 1],
        grad_output[0, 1],
    )
    normed = jnp.stack([producer[0], consumer[0]])[None]
    grad_q = jnp.stack([producer[1], consumer[1]])[None]
    own_sum = lax.psum_scatter(
        producer[2].astype(jnp.bfloat16), "ctx", scatter_dimension=0, tiled=True
    ).astype(jnp.float32)
    their_sum = lax.psum_scatter(
        consumer[2].astype(jnp.bfloat16), "ctx", scatter_dimension=0, tiled=True
    ).astype(jnp.float32)
    kv_grad = own_sum + passed_along(their_sum.astype(jnp.bfloat16), "section", -1).astype(
        their_sum.dtype
    )
    return (normed, grad_q, kv_grad[None])


def layer_kernel(
    bounds, q_ref, k_ref, v_ref, g_ref, gain_ref, limit_ref,
    normed_ref, dq_ref, dk_ref, dv_ref,
    weights, scores, outs, recip, q_t, stack, grad_t, total, dots,
):
    phase, head = pl.program_id(0), pl.program_id(1)
    seq_len = k_ref.shape[0]
    rows = q_ref.shape[0]
    wide = GROUP * rows
    span = scores.shape[1]
    blocks = seq_len // span
    full, some = bounds[0], bounds[1]
    scaling = HD ** (-0.5)
    log_scale = scaling * LOG2E
    features = q_ref.shape[1] * pl.num_programs(1)

    for g in range(GROUP):
        part = q_ref[:, g * HD:(g + 1) * HD]
        q_t[:, g * rows:(g + 1) * rows] = part.T
        stack[g * rows:(g + 1) * rows, :] = part

    @pl.when(phase == 0)
    def _():
        @pl.when(head == 0)
        def _():
            dots[...] = jnp.zeros_like(dots)

        def folded(found):
            return jnp.max(found.reshape(span // 8, 8, wide), axis=0)

        def plain(c, top):
            found = dot_nn(k_ref[pl.ds(c * span, span), :], q_t[...])
            scores[c] = found
            return jnp.maximum(top, folded(found))

        def masked(c, top):
            found = dot_nn(k_ref[pl.ds(c * span, span), :], q_t[...])
            place = c * span + lax.broadcasted_iota(jnp.int32, (span, wide), 0)
            found = jnp.where(place <= limit_ref[...], found, neg_big)
            scores[c] = found
            return jnp.maximum(top, folded(found))

        top = jnp.full((8, wide), neg_big, jnp.float32)
        top = lax.fori_loop(0, full, plain, top)
        top = lax.fori_loop(full, some, masked, top)
        top = jnp.max(top, axis=0, keepdims=True) * log_scale
        total[...] = jnp.zeros_like(total)
        ones = jnp.ones((16, span), jnp.bfloat16)

        def weigh(c, carry):
            at = pl.ds(c * span, span)
            found = jnp.exp2(scores[c] * log_scale - top).astype(jnp.bfloat16)
            weights[head, at, :] = found
            values = jnp.concatenate([v_ref[at, :].T, ones], axis=0)
            total[...] += dot_nn(values, found)
            return carry

        lax.fori_loop(0, some, weigh, 0)
        inverse = 1.0 / total[HD:HD + 1, :]
        recip[head] = jnp.broadcast_to(inverse, (8, wide))
        out = total[:HD, :] * inverse
        outs[head] = out
        square, cross = dots[0], dots[1]
        for g in range(GROUP):
            part = out[:, g * rows:(g + 1) * rows].T
            scaled = g_ref[:, g * HD:(g + 1) * HD].astype(jnp.float32) * gain_ref[:, g * HD:(g + 1) * HD]
            square = square + part * part
            cross = cross + scaled * part
        dots[0], dots[1] = square, cross

    @pl.when(phase == 1)
    def _():
        square = jnp.sum(dots[0], axis=-1, keepdims=True) / features
        center = jnp.sum(dots[1], axis=-1, keepdims=True) / features
        inverse = lax.rsqrt(square + eps_norm)
        pull = inverse * inverse * center
        row_dot = []
        for g in range(GROUP):
            cols, lanes = slice(g * HD, (g + 1) * HD), slice(g * rows, (g + 1) * rows)
            part_t = outs[head, :, lanes]
            part = part_t.T
            gain = gain_ref[:, cols]
            normed_ref[:, cols] = (part * inverse * gain).astype(jnp.bfloat16)
            scaled = g_ref[:, cols].astype(jnp.float32) * gain
            grad = inverse * (scaled - part * pull)
            turned = (grad.T * recip[head, 0:1, lanes]).astype(jnp.bfloat16)
            grad_t[:, lanes] = turned
            row_dot.append(jnp.sum(turned.astype(jnp.float32) * part_t, axis=0, keepdims=True))
        row_dot = jnp.concatenate(row_dot, axis=1)
        total[...] = jnp.zeros_like(total)

        def back(c, carry):
            at = pl.ds(c * span, span)
            chances = weights[head, at, :]
            dv_ref[at, :] = dot_nt(chances, grad_t[...]).astype(jnp.bfloat16)
            moved = dot_nn(v_ref[at, :], grad_t[...]) - row_dot
            moved = (chances.astype(jnp.float32) * moved).astype(jnp.bfloat16)
            dk_ref[at, :] = (dot_nn(moved, stack[...]) * scaling).astype(jnp.bfloat16)
            total[:HD, :] += dot_nn(k_ref[at, :].T, moved)
            return carry

        lax.fori_loop(0, some, back, 0)

        def empty(c, carry):
            at = pl.ds(c * span, span)
            dk_ref[at, :] = jnp.zeros((span, HD), jnp.bfloat16)
            dv_ref[at, :] = jnp.zeros((span, HD), jnp.bfloat16)
            return carry

        lax.fori_loop(some, blocks, empty, 0)
        for g in range(GROUP):
            part = total[:HD, g * rows:(g + 1) * rows].T * scaling
            dq_ref[:, g * HD:(g + 1) * HD] = part.astype(jnp.bfloat16)


def run_layer_kernel(queries, kv, gain, cotangent, limit, bounds):
    rows = queries.shape[0]
    seq_len, heads = kv.shape[0], kv.shape[1] // (2 * HD)
    span = min(SPAN, seq_len)
    wide = GROUP * rows
    by_head = lambda p, h, b: (0, h)
    second = lambda p, h, b: (0, p * h)
    spec = pl.BlockSpec
    return pl.pallas_call(
        layer_kernel,
        grid_spec=pltpu.PrefetchScalarGridSpec(
            num_scalar_prefetch=1,
            grid=(2, heads),
            in_specs=[
                spec((rows, GROUP * HD), by_head),
                spec((seq_len, HD), by_head),
                spec((seq_len, HD), lambda p, h, b: (0, heads + h)),
                spec((rows, GROUP * HD), by_head),
                spec((1, GROUP * HD), by_head),
                spec((1, wide), lambda p, h, b: (0, 0)),
            ],
            out_specs=[
                spec((rows, GROUP * HD), second),
                spec((rows, GROUP * HD), second),
                spec((seq_len, HD), second),
                spec((seq_len, HD), second),
            ],
            scratch_shapes=[
                pltpu.VMEM((heads, seq_len, wide), jnp.bfloat16),
                pltpu.VMEM((seq_len // span, span, wide), jnp.float32),
                pltpu.VMEM((heads, HD, wide), jnp.float32),
                pltpu.VMEM((heads, 8, wide), jnp.float32),
                pltpu.VMEM((HD, wide), jnp.bfloat16),
                pltpu.VMEM((wide, HD), jnp.bfloat16),
                pltpu.VMEM((HD, wide), jnp.bfloat16),
                pltpu.VMEM((HD + 16, wide), jnp.float32),
                pltpu.VMEM((2, rows, HD), jnp.float32),
            ],
        ),
        out_shape=[
            jax.ShapeDtypeStruct(queries.shape, jnp.bfloat16),
            jax.ShapeDtypeStruct(queries.shape, jnp.bfloat16),
            jax.ShapeDtypeStruct((seq_len, heads * HD), jnp.bfloat16),
            jax.ShapeDtypeStruct((seq_len, heads * HD), jnp.bfloat16),
        ],
        compiler_params=pltpu.CompilerParams(vmem_limit_bytes=56 * 1024 * 1024),
        cost_estimate=pl.CostEstimate(
            flops=12 * wide * seq_len * HD * heads,
            bytes_accessed=32 * 1024 * 1024,
            transcendentals=wide * seq_len * heads,
        ),
    )(bounds, queries, kv, kv, cotangent, gain, limit)


def on_device_kernel(query_heads, keys_values, grad_output, norm_gain, turn_ids):
    rows = turn_ids.shape[0]
    first = lax.axis_index("ctx") * rows
    own = keys_values[0].reshape(rows, -1)
    key_turns = lax.all_gather(turn_ids, "ctx", axis=0, tiled=True)
    earlier = passed_along(own, "section", 1)
    own_full = lax.all_gather(own, "ctx", axis=0, tiled=True)
    earlier_full = lax.all_gather(earlier, "ctx", axis=0, tiled=True)
    limit = jnp.sum((key_turns[None, :] <= turn_ids[:, None]).astype(jnp.int32), axis=1) - 1
    span = min(SPAN, key_turns.shape[0])
    bounds = jnp.stack([(first + 1) // span, jnp.max(limit) // span + 1]).astype(jnp.int32)
    limit = jnp.tile(limit, GROUP)[None, :]
    results = [
        run_layer_kernel(
            query_heads[0, p], full, norm_gain[0, p][None, :], grad_output[0, p], limit, bounds
        )
        for p, full in enumerate((own_full, earlier_full))
    ]
    sums = [
        lax.psum_scatter(
            jnp.concatenate([r[2], r[3]], axis=1), "ctx", scatter_dimension=0, tiled=True
        )
        for r in results
    ]
    kv_grad = sums[0].astype(jnp.float32) + passed_along(sums[1], "section", -1).astype(jnp.float32)
    normed = jnp.stack([results[0][0], results[1][0]])[None]
    grad_q = jnp.stack([results[0][1], results[1][1]])[None]
    return (normed, grad_q, kv_grad.reshape(keys_values.shape))


def solution(mesh):
    in_specs = (
        P("section", None, "ctx", "tp"),
        P("section", "ctx", None, "tp"),
        P("section", None, "ctx", "tp"),
        P("section", None, "tp"),
        P("ctx"),
    )
    out_specs = (
        P("section", None, "ctx", "tp"),
        P("section", None, "ctx", "tp"),
        P("section", "ctx", None, "tp"),
    )
    body = on_device_kernel if mesh.shape["tp"] == 1 else on_device
    return jax.shard_map(
        body, mesh=mesh, in_specs=in_specs, out_specs=out_specs, check_vma=False
    )
```

```python
import jax
import jax.numpy as jnp
from jax import lax
from jax.experimental import pallas as pl
from jax.experimental.pallas import tpu as pltpu
from jax.sharding import PartitionSpec as P

HD = 128
KVH = 8
GROUP = 6


neg_big = -1e30
eps_norm = 1e-06
LOG2E = 1.4426950408889634
SPAN = 512


def dot_nn(a, b):
    return jnp.dot(a, b, preferred_element_type=jnp.float32)


def dot_nt(a, b):
    return lax.dot_general(a, b, (((1,), (1,)), ((), ())), preferred_element_type=jnp.float32)


def passed_along(block, axis, distance):
    devices = range(lax.axis_size(axis))
    route = [((i - distance) % len(devices), i) for i in devices]
    return lax.ppermute(block, axis, route)


def visible_mask(query_pos, query_seg, key_pos, key_seg):
    return (key_pos[None, :] <= query_pos[:, None]) | (key_seg[None, :] == query_seg[:, None])


def block_terms(queries, kv_rows, scaling):
    row_count = kv_rows.shape[0]
    head_count = queries.shape[1]
    key_rows = kv_rows[:, 0].reshape(row_count, head_count, HD)
    value_rows = kv_rows[:, 1].reshape(row_count, head_count, HD)
    scores = (
        jnp.einsum("qhgd,khd->hgqk", queries, key_rows, preferred_element_type=jnp.float32)
        * scaling
    )
    return (scores, key_rows, value_rows)


def run_layer(queries_flat, gathered, key_seg, query_pos, query_seg, gain_vector, cotangent_flat):
    tokens_here = queries_flat.shape[0]
    head_count = gathered.shape[2] // HD
    queries = queries_flat.reshape(tokens_here, head_count, GROUP, HD)
    scaling = HD ** (-0.5)
    seq_len = gathered.shape[0]
    span_rows = min(512, seq_len)
    blocks = seq_len // span_rows

    def block_view(number):
        offset = number * span_rows
        kv_rows = lax.dynamic_slice_in_dim(gathered, offset, span_rows, 0)
        key_pos = offset + jnp.arange(span_rows, dtype=jnp.int32)
        visible = visible_mask(
            query_pos, query_seg, key_pos, lax.dynamic_slice_in_dim(key_seg, offset, span_rows, 0)
        )
        scores, key_rows, value_rows = block_terms(queries, kv_rows, scaling)
        return (scores, key_rows, value_rows, visible)

    def forward_step(running, number):
        run_max, run_sum, accumulated = running
        scores, key_rows, value_rows, visible = block_view(number)
        new_max = jnp.maximum(run_max, jnp.max(jnp.where(visible, scores, neg_big), axis=-1))
        weights = jnp.where(visible, jnp.exp(scores - new_max[..., None]), 0.0)
        factor = jnp.exp(run_max - new_max)
        run_sum = run_sum * factor + jnp.sum(weights, axis=-1)
        update = jnp.einsum(
            "hgqk,khd->qhgd",
            weights.astype(jnp.bfloat16),
            value_rows,
            preferred_element_type=jnp.float32,
        )
        accumulated = accumulated * jnp.transpose(factor, (2, 0, 1))[..., None] + update
        return ((new_max, run_sum, accumulated), None)

    start_state = (
        jnp.full((head_count, GROUP, tokens_here), neg_big, jnp.float32),
        jnp.zeros((head_count, GROUP, tokens_here), jnp.float32),
        jnp.zeros((tokens_here, head_count, GROUP, HD), jnp.float32),
    )
    (row_max, row_sum, accumulated), unused = lax.scan(
        forward_step, start_state, jnp.arange(blocks, dtype=jnp.int32)
    )
    output = accumulated / jnp.transpose(row_sum, (2, 0, 1))[..., None]
    gain_grid = gain_vector.reshape(head_count, GROUP, HD)
    scaled = (
        cotangent_flat.reshape(tokens_here, head_count, GROUP, HD).astype(jnp.float32) * gain_grid
    )
    local_sq = jnp.sum(output * output, axis=(1, 2, 3))
    local_dot = jnp.sum(scaled * output, axis=(1, 2, 3))
    total_sq, total_dot = lax.psum((local_sq, local_dot), "tp")
    features = KVH * GROUP * HD
    inverse = lax.rsqrt(total_sq / features + eps_norm)
    normed = (output * inverse[:, None, None, None] * gain_grid).astype(jnp.bfloat16)
    center = total_dot / features
    out_grad = (
        inverse[:, None, None, None]
        * (scaled - output * (inverse * inverse * center)[:, None, None, None])
    ).astype(jnp.bfloat16)
    row_dot = jnp.transpose(jnp.sum(out_grad.astype(jnp.float32) * output, axis=-1), (1, 2, 0))

    def backward_step(grad_q, number):
        scores, key_rows, value_rows, visible = block_view(number)
        chances = jnp.where(visible, jnp.exp(scores - row_max[..., None]), 0.0) / row_sum[..., None]
        value_grad = jnp.einsum(
            "hgqk,qhgd->khd",
            chances.astype(jnp.bfloat16),
            out_grad,
            preferred_element_type=jnp.float32,
        )
        prob_grad = jnp.einsum(
            "qhgd,khd->hgqk", out_grad, value_rows, preferred_element_type=jnp.float32
        )
        score_grad = (chances * (prob_grad - row_dot[..., None])).astype(jnp.bfloat16)
        grad_q = (
            grad_q
            + jnp.einsum("hgqk,khd->qhgd", score_grad, key_rows, preferred_element_type=jnp.float32)
            * scaling
        )
        key_grad = (
            jnp.einsum("hgqk,qhgd->khd", score_grad, queries, preferred_element_type=jnp.float32)
            * scaling
        )
        return (grad_q, jnp.stack([key_grad, value_grad], axis=1))

    grad_q, pieces = lax.scan(
        backward_step,
        jnp.zeros((tokens_here, head_count, GROUP, HD), jnp.float32),
        jnp.arange(blocks, dtype=jnp.int32),
    )
    kv_partial = pieces.reshape(seq_len, 2, head_count * HD)
    return (
        normed.reshape(tokens_here, -1),
        grad_q.reshape(tokens_here, -1).astype(jnp.bfloat16),
        kv_partial,
    )


def on_device(query_heads, keys_values, grad_output, norm_gain, turn_ids):
    tokens_here = turn_ids.shape[0]
    query_pos = lax.axis_index("ctx") * tokens_here + jnp.arange(tokens_here, dtype=jnp.int32)
    own_rows = keys_values[0]
    earlier = passed_along(own_rows, "section", 1)
    own_full, key_seg = (
        lax.all_gather(own_rows, "ctx", axis=0, tiled=True),
        lax.all_gather(turn_ids, "ctx", axis=0, tiled=True),
    )
    earlier_full = lax.all_gather(earlier, "ctx", axis=0, tiled=True)
    producer = run_layer(
        query_heads[0, 0],
        own_full,
        key_seg,
        query_pos,
        turn_ids,
        norm_gain[0, 0],
        grad_output[0, 0],
    )
    consumer = run_layer(
        query_heads[0, 1],
        earlier_full,
        key_seg,
        query_pos,
        turn_ids,
        norm_gain[0, 1],
        grad_output[0, 1],
    )
    normed = jnp.stack([producer[0], consumer[0]])[None]
    grad_q = jnp.stack([producer[1], consumer[1]])[None]
    own_sum = lax.psum_scatter(
        producer[2].astype(jnp.bfloat16), "ctx", scatter_dimension=0, tiled=True
    ).astype(jnp.float32)
    their_sum = lax.psum_scatter(
        consumer[2].astype(jnp.bfloat16), "ctx", scatter_dimension=0, tiled=True
    ).astype(jnp.float32)
    kv_grad = own_sum + passed_along(their_sum.astype(jnp.bfloat16), "section", -1).astype(
        their_sum.dtype
    )
    return (normed, grad_q, kv_grad[None])


def layer_kernel(
    bounds, q_ref, mine_ref, other_ref, g_ref, gain_ref, limit_ref,
    normed_ref, dq_ref, keep_ref, send_ref,
    weights, scores, outs, recip, q_t, stack, grad_t, total, dots,
):
    phase, head = pl.program_id(0), pl.program_id(1)
    half = mine_ref.shape[0]
    key_cols, value_cols = slice(0, HD), slice(HD, 2 * HD)
    rows = q_ref.shape[0]
    wide = GROUP * rows
    span = scores.shape[1]
    blocks = half // span
    side = bounds[4]
    sides = ((mine_ref, keep_ref, side, 0), (other_ref, send_ref, 1 - side, 1))
    scaling = HD ** (-0.5)
    log_scale = scaling * LOG2E
    features = q_ref.shape[1] * pl.num_programs(1)

    for g in range(GROUP):
        part = q_ref[:, g * HD:(g + 1) * HD]
        q_t[:, g * rows:(g + 1) * rows] = part.T
        stack[g * rows:(g + 1) * rows, :] = part

    @pl.when(phase == 0)
    def _():
        @pl.when(head == 0)
        def _():
            dots[...] = jnp.zeros_like(dots)

        def folded(found):
            return jnp.max(found.reshape(span // 8, 8, wide), axis=0)

        top = jnp.full((8, wide), neg_big, jnp.float32)
        for kv_ref, _, parity, u in sides:
            def found_at(c):
                return dot_nn(kv_ref[pl.ds(c * span, span), key_cols], q_t[...])

            def plain(c, top):
                found = found_at(c)
                scores[u * blocks + c] = found
                return jnp.maximum(top, folded(found))

            def masked(c, top):
                line = lax.broadcasted_iota(jnp.int32, (rows, wide), 0)
                place = jnp.concatenate([line + 2 * rows * k for k in range(span // rows)], axis=0)
                start = 2 * c * span + parity * rows
                found = jnp.where(place <= limit_ref[...] - start, found_at(c), neg_big)
                scores[u * blocks + c] = found
                return jnp.maximum(top, folded(found))

            top = lax.fori_loop(0, bounds[2 * u], plain, top)
            top = lax.fori_loop(bounds[2 * u], bounds[2 * u + 1], masked, top)
        top = jnp.max(top, axis=0, keepdims=True) * log_scale
        total[...] = jnp.zeros_like(total)
        ones = jnp.ones((16, span), jnp.bfloat16)

        for kv_ref, _, _, u in sides:
            def weigh(c, carry):
                found = jnp.exp2(scores[u * blocks + c] * log_scale - top).astype(jnp.bfloat16)
                weights[head, u * blocks + c] = found
                values = jnp.concatenate([kv_ref[pl.ds(c * span, span), value_cols].T, ones], axis=0)
                total[...] += dot_nn(values, found)
                return carry

            lax.fori_loop(0, bounds[2 * u + 1], weigh, 0)
        inverse = 1.0 / total[HD:HD + 1, :]
        recip[head] = jnp.broadcast_to(inverse, (8, wide))
        out = total[:HD, :] * inverse
        outs[head] = out
        square, cross = dots[0], dots[1]
        for g in range(GROUP):
            part = out[:, g * rows:(g + 1) * rows].T
            scaled = g_ref[:, g * HD:(g + 1) * HD].astype(jnp.float32) * gain_ref[:, g * HD:(g + 1) * HD]
            square = square + part * part
            cross = cross + scaled * part
        dots[0], dots[1] = square, cross

    @pl.when(phase == 1)
    def _():
        square = jnp.sum(dots[0], axis=-1, keepdims=True) / features
        center = jnp.sum(dots[1], axis=-1, keepdims=True) / features
        inverse = lax.rsqrt(square + eps_norm)
        pull = inverse * inverse * center
        row_dot = []
        for g in range(GROUP):
            cols, lanes = slice(g * HD, (g + 1) * HD), slice(g * rows, (g + 1) * rows)
            part_t = outs[head, :, lanes]
            part = part_t.T
            gain = gain_ref[:, cols]
            normed_ref[:, cols] = (part * inverse * gain).astype(jnp.bfloat16)
            scaled = g_ref[:, cols].astype(jnp.float32) * gain
            grad = inverse * (scaled - part * pull)
            turned = (grad.T * recip[head, 0:1, lanes]).astype(jnp.bfloat16)
            grad_t[:, lanes] = turned
            row_dot.append(jnp.sum(turned.astype(jnp.float32) * part_t, axis=0, keepdims=True))
        row_dot = jnp.concatenate(row_dot, axis=1)
        total[...] = jnp.zeros_like(total)

        for kv_ref, grad_ref, _, u in sides:
            def back(c, carry):
                at = pl.ds(c * span, span)
                chances = weights[head, u * blocks + c]
                grad_ref[at, value_cols] = dot_nt(chances, grad_t[...]).astype(jnp.bfloat16)
                moved = dot_nn(kv_ref[at, value_cols], grad_t[...]) - row_dot
                moved = (chances.astype(jnp.float32) * moved).astype(jnp.bfloat16)
                grad_ref[at, key_cols] = (dot_nn(moved, stack[...]) * scaling).astype(jnp.bfloat16)
                total[:HD, :] += dot_nn(kv_ref[at, key_cols].T, moved)
                return carry

            def empty(c, carry):
                grad_ref[pl.ds(c * span, span), :] = jnp.zeros((span, 2 * HD), jnp.bfloat16)
                return carry

            lax.fori_loop(0, bounds[2 * u + 1], back, 0)
            lax.fori_loop(bounds[2 * u + 1], blocks, empty, 0)
        for g in range(GROUP):
            part = total[:HD, g * rows:(g + 1) * rows].T * scaling
            dq_ref[:, g * HD:(g + 1) * HD] = part.astype(jnp.bfloat16)


def run_layer_kernel(layer, queries, mine, other, gain, cotangent, limit, bounds, span):
    rows = queries.shape[2]
    half, heads = mine.shape[0], mine.shape[1] // (2 * HD)
    seq_len = 2 * half
    wide = GROUP * rows
    whole = lambda p, h, b: (0, layer, 0, h)
    by_head = lambda p, h, b: (0, h)
    second = lambda p, h, b: (0, p * h)
    spec = pl.BlockSpec
    flat = (rows, queries.shape[3])
    return pl.pallas_call(
        layer_kernel,
        grid_spec=pltpu.PrefetchScalarGridSpec(
            num_scalar_prefetch=1,
            grid=(2, heads),
            in_specs=[
                spec((None, None, rows, GROUP * HD), whole),
                spec((half, 2 * HD), by_head),
                spec((half, 2 * HD), by_head),
                spec((None, None, rows, GROUP * HD), whole),
                spec((1, GROUP * HD), by_head),
                spec((1, wide), lambda p, h, b: (0, 0)),
            ],
            out_specs=[
                spec((rows, GROUP * HD), second),
                spec((rows, GROUP * HD), second),
                spec((half, 2 * HD), second),
                spec((half, 2 * HD), second),
            ],
            scratch_shapes=[
                pltpu.VMEM((heads, seq_len // span, span, wide), jnp.bfloat16),
                pltpu.VMEM((seq_len // span, span, wide), jnp.float32),
                pltpu.VMEM((heads, HD, wide), jnp.float32),
                pltpu.VMEM((heads, 8, wide), jnp.float32),
                pltpu.VMEM((HD, wide), jnp.bfloat16),
                pltpu.VMEM((wide, HD), jnp.bfloat16),
                pltpu.VMEM((HD, wide), jnp.bfloat16),
                pltpu.VMEM((HD + 16, wide), jnp.float32),
                pltpu.VMEM((2, rows, HD), jnp.float32),
            ],
        ),
        out_shape=[
            jax.ShapeDtypeStruct(flat, jnp.bfloat16),
            jax.ShapeDtypeStruct(flat, jnp.bfloat16),
            jax.ShapeDtypeStruct(mine.shape, jnp.bfloat16),
            jax.ShapeDtypeStruct(mine.shape, jnp.bfloat16),
        ],
        compiler_params=pltpu.CompilerParams(vmem_limit_bytes=56 * 1024 * 1024),
        cost_estimate=pl.CostEstimate(
            flops=12 * wide * seq_len * HD * heads,
            bytes_accessed=32 * 1024 * 1024,
            transcendentals=wide * seq_len * heads,
        ),
    )(bounds, queries, mine, other, cotangent, gain, limit)


def on_device_kernel(query_heads, keys_values, grad_output, norm_gain, turn_ids):
    rows = turn_ids.shape[0]
    width = lax.axis_size("ctx")
    here = lax.axis_index("ctx")
    side = lax.rem(here, 2)
    first = here * rows
    teams = [list(range(start, width, 2)) for start in range(2)]
    pairs = [(i, i + 1 - 2 * (i % 2)) for i in range(width)]
    heads = keys_values.shape[3] // HD
    own = keys_values.reshape(rows, 2, heads, HD).transpose(0, 2, 1, 3).reshape(rows, -1)

    def gathered(block):
        mine = lax.all_gather(block, "ctx", axis=0, tiled=True, axis_index_groups=teams)
        return (mine, lax.ppermute(mine, "ctx", pairs))

    def spread(keep, send):
        came = lax.ppermute(send, "ctx", pairs)
        both = (keep.astype(jnp.float32) + came.astype(jnp.float32)).astype(jnp.bfloat16)
        return lax.psum_scatter(
            both, "ctx", scatter_dimension=0, tiled=True, axis_index_groups=teams
        )

    later = jnp.where(here + 1 < width, passed_along(turn_ids, "ctx", -1), -1)
    earlier = passed_along(own, "section", 1)
    reach = (turn_ids[None, :] <= turn_ids[:, None]).astype(jnp.int32)
    reach = reach + (later[None, :] == turn_ids[:, None]).astype(jnp.int32)
    limit = first + jnp.sum(reach, axis=1) - 1
    half = rows * width // 2
    span = SPAN if half % SPAN == 0 and SPAN % rows == 0 else half
    starts = 2 * span * jnp.arange(half // span, dtype=jnp.int32)
    bounds = []
    for parity in (side, 1 - side):
        lowest = starts + parity * rows
        highest = lowest + 2 * span - rows - 1
        bounds += [jnp.sum(highest <= first), jnp.sum(lowest <= jnp.max(limit))]
    bounds = jnp.stack(bounds + [side]).astype(jnp.int32)
    limit = jnp.tile(limit, GROUP)[None, :]
    results = [
        run_layer_kernel(
            p, query_heads, *gathered(block), norm_gain[0, p][None, :], grad_output, limit, bounds, span
        )
        for p, block in enumerate((own, earlier))
    ]
    sums = [spread(r[2], r[3]) for r in results]
    kv_grad = sums[0].astype(jnp.float32) + passed_along(sums[1], "section", -1).astype(jnp.float32)
    kv_grad = kv_grad.reshape(rows, heads, 2, HD).transpose(0, 2, 1, 3)
    normed = jnp.stack([results[0][0], results[1][0]])[None]
    grad_q = jnp.stack([results[0][1], results[1][1]])[None]
    return (normed, grad_q, kv_grad.reshape(keys_values.shape))


def solution(mesh):
    in_specs = (
        P("section", None, "ctx", "tp"),
        P("section", "ctx", None, "tp"),
        P("section", None, "ctx", "tp"),
        P("section", None, "tp"),
        P("ctx"),
    )
    out_specs = (
        P("section", None, "ctx", "tp"),
        P("section", None, "ctx", "tp"),
        P("section", "ctx", None, "tp"),
    )
    fits = mesh.shape["tp"] == 1 and mesh.shape["ctx"] % 2 == 0
    body = on_device_kernel if fits else on_device
    return jax.shard_map(
        body, mesh=mesh, in_specs=in_specs, out_specs=out_specs, check_vma=False
    )
```
